512 devices in a mesh: group: 32 (over z, core), member: 16 (over y, x).
Axes of the slice: x: 4, y: 4, z: 16, core: 2. Of those that a mesh axis runs over, the one named last changes fastest.
Arguments:
- route_group: int32 [2048, 4], P('group'), may hold values from 0 to 31, all different within a row; in each aligned block of 64 rows (0 to 63, 64 to 127, ...) at most 10 rows name the same one
- expert_pick: int32 [2048, 4, 2], P('group'), may hold values 0 or 1
- route_score: float32 [2048, 4, 2], P('group'), may hold values from 0.1 to 1
- expert_hidden: bfloat16 [32, 320, 4096], P('group', 'member'), may hold values from -6 to 6
- down_weight: bfloat16 [32, 2, 2048, 7168], P('group', None, None, 'member'), may hold values from -0.125 to 0.125
Outputs:
- combined: bfloat16 [2048, 7168], P('group', 'member')
The draws below stay inside these ranges and needn't reach their ends.
Inputs may be any that keep to these rules, and one draw needn't show every extreme that they name: `route_group`: within the 64 tokens of one home group (aligned blocks of rows) a token's 4 groups differ, no group is chosen by more than 10 tokens, a bound that some block reaches.
All inputs are finite; a program needn't handle non-finite values. No bound on the sum of `expert_pick` on one device may be relied on, other than what follows from the above.
Results may differ from the reference program's by a relative error of at most 0.001.
Values may be sent and summed in bfloat16 or wider, within the bound.
A program may use at most 64 MiB of HBM per device.

```python
import math
import jax
import jax.numpy as jnp
import numpy as np
from jax import lax

D = 7168
FF = 2048
EXP_G = 2
TOPG = 4
TOK_G = 64
CAPS = 10
TOKENS = 2048
N_GROUP = 32


def place_ends(values, stream_key, least, top_value):
    index_at = [jax.random.randint(jax.random.fold_in(stream_key, axis), (), 0, length) for axis, length in enumerate(values.shape)]
    widest = values.shape.index(max(values.shape))
    neighbour = index_at[:widest] + [(index_at[widest] + 1) % values.shape[widest]] + index_at[widest + 1:]
    return values.at[tuple(index_at)].set(least).at[tuple(neighbour)].set(top_value)


def block_levels(rng, dims, cuts, least, high):
    def one(position, blocks):
        steps = jax.random.uniform(jax.random.fold_in(jax.random.fold_in(rng, 6), position), (blocks,), jnp.float32, least / len(cuts), high / len(cuts))
        return jnp.repeat(jnp.exp(steps), dims[position] // blocks).reshape((-1,) + (1,) * (len(dims) - position - 1))

    loudness = one(*cuts[0])
    for cut in cuts[1:]:
        loudness = loudness * one(*cut)
    return loudness


def deal_out(key, own, number, rows, amount, top, bound, lean):
    order = jax.random.permutation(key, amount)
    crowded, ordinary = load_shares(amount, rows * top, bound, lean, True), load_shares(amount, rows * top, bound, lean, False)
    places = jnp.arange(amount)

    def named(tallies, offset_by):
        used = int((tallies > 0).sum())
        fixed = max(1, used // 4)
        moved = fixed + (places - fixed + offset_by * (used - fixed)) % max(1, amount - fixed)
        return jnp.zeros((amount,), jnp.int32).at[order[jnp.where(places < fixed, places, moved)]].set(jnp.asarray(tallies, jnp.int32))

    tallies = jnp.where(number % 4 == 0, named(crowded, number // 4), named(ordinary, number - number // 4 - 1))
    mixed = jax.random.permutation(jax.random.fold_in(own, 3), amount)
    donor, taker = mixed[0:amount // 2 * 2:2], mixed[1:amount // 2 * 2:2]
    slack = jnp.minimum(tallies[donor] - 1, bound - tallies[taker]) // 2
    slack = jnp.where((donor == order[0]) | (taker == order[0]) | (tallies[taker] == 0), 0, jnp.maximum(slack, 0))
    moved = jax.random.randint(jax.random.fold_in(own, 4), (amount // 2,), 0, 1 << 20) % (slack + 1)
    tallies = tallies.at[donor].add(-moved).at[taker].add(moved)
    items = jnp.searchsorted(jnp.cumsum(tallies), jnp.arange(rows * top), side="right").astype(jnp.int32)
    listing = items.reshape(top, rows).T
    listing = listing[jax.random.permutation(jax.random.fold_in(own, 1), rows)]
    offset_by = jax.random.randint(jax.random.fold_in(own, 2), (rows, 1), 0, top)
    return jnp.take_along_axis(listing, (jnp.arange(top)[None, :] + offset_by) % top, axis=1)


def load_shares(number_of, total, bound, skew, full):
    loads = [(1 << 20) // math.isqrt(grade ** skew) + 1 for grade in range(1, number_of + 1)]
    largest = bound if full else min(bound, max(-(-total // number_of), total * loads[0] // sum(loads)))
    least = 1 if total - largest >= number_of - 1 else 0
    counts, rest = [largest] + [least] * (number_of - 1), total - largest - least * (number_of - 1)
    while rest > 0:
        free = [i for i in range(1, number_of) if counts[i] < largest] or [i for i in range(1, number_of) if counts[i] < bound]
        mass, budget = sum([loads[i] for i in free]), rest
        for i in free:
            extra = min(bound - counts[i], max(1, budget * loads[i] // mass), rest)
            counts[i] = counts[i] + extra
            rest = rest - extra
    return np.array(counts)


def scatter_about(rng, dims, scale, bound, split=(), kind=jnp.bfloat16):
    level = block_levels(rng, dims, split, -0.22, 0.18) if split else 1.0
    result = jax.random.normal(rng, dims, jnp.float32) * scale * level
    return jnp.minimum(jnp.maximum(result, -bound), bound).astype(kind)


def setup_inputs(seed: int = 0) -> dict:
    key_list = jax.random.split(jax.random.key(seed), 6)
    route_group_keys = jax.random.split(jax.random.fold_in(key_list[0], 1), TOKENS // TOK_G)
    route_group_turns = jax.random.permutation(jax.random.fold_in(key_list[0], 3), TOKENS // TOK_G)
    route_group = jax.vmap(lambda own, number: deal_out(jax.random.fold_in(key_list[0], 2), own, number, TOK_G, N_GROUP, TOPG, CAPS, 2))(route_group_keys, route_group_turns).reshape((TOKENS, TOPG))
    expert_pick = place_ends((jax.random.randint(key_list[1], (TOKENS, TOPG, EXP_G), 0, 4) < 3).astype(jnp.int32), jax.random.fold_in(key_list[1], 1), 0, 1)
    route_score = jnp.clip(jnp.exp(math.log(1.0) - 2.3025851 * jax.random.uniform(key_list[2], (TOKENS, TOPG, EXP_G), jnp.float32) ** block_levels(key_list[2], (TOKENS, TOPG, EXP_G), ((0, 32),), -0.2, 0.2)), 0.1, 1.0)
    expert_hidden = scatter_about(key_list[3], (N_GROUP, N_GROUP * CAPS, EXP_G * FF), 1.0, 6.0, ((0, 32), (1, 16)))
    down_weight = scatter_about(key_list[4], (N_GROUP, EXP_G, FF, D), FF ** -0.5, 0.125, ((0, 32), (3, 16)))
    return dict(route_group=route_group, expert_pick=expert_pick, route_score=route_score, expert_hidden=expert_hidden, down_weight=down_weight)


def slot_positions(route_group):
    chosen = route_group.reshape(N_GROUP, TOK_G, TOPG)
    labels = jnp.arange(N_GROUP, dtype=jnp.int32)
    onehot = (chosen[..., None] == labels).astype(jnp.int32)
    per_token = jnp.sum(onehot, axis=2)
    earlier = jnp.cumsum(per_token, axis=1) - per_token
    slot_rank = jnp.take_along_axis(earlier, chosen, axis=2)
    home_group = jnp.arange(N_GROUP, dtype=jnp.int32)[:, None, None]
    return chosen, (home_group * CAPS + slot_rank).astype(jnp.int32)


def reference(route_group, expert_pick, route_score, expert_hidden, down_weight):
    chosen, slot_row = slot_positions(route_group)
    coef = (route_score * expert_pick.astype(jnp.float32)).reshape(N_GROUP, TOK_G, TOPG, EXP_G)
    slot_coef = jnp.zeros((N_GROUP, N_GROUP * CAPS, EXP_G), jnp.float32).at[chosen, slot_row].set(coef)

    def one_group(packed):
        hidden, weight, table = packed
        total = jnp.zeros((hidden.shape[0], D), jnp.float32)
        for expert in range(EXP_G):
            product = jnp.dot(hidden[:, expert * FF:(expert + 1) * FF], weight[expert], preferred_element_type=jnp.float32)
            total = total + table[:, expert:expert + 1] * product
        return total

    slot_out = lax.map(one_group, (expert_hidden, down_weight, slot_coef))
    picked = slot_out[chosen, slot_row]
    combined = jnp.sum(picked, axis=2).astype(jnp.bfloat16)
    return combined.reshape(TOKENS, D)
```

```python
import functools

import jax
import jax.numpy as jnp
from jax import lax
from jax.experimental import pallas as pl
from jax.experimental.pallas import tpu as pltpu
from jax.sharding import PartitionSpec as P

MESH = pl.DeviceIdType.MESH
NG = 32
NM = 16
ROWS = 8
WIDE = 5120
HALF = WIDE // 2
LANES = 128
MAIN = 64

BATCHES = (
    ((0, 0), (1, 0), (3, 0)),
    ((2, 0), (0, 1), (0, 3)),
    ((1, 1), (3, 1), (1, 3), (3, 3)),
    ((2, 1), (2, 3), (0, 2)),
    ((1, 2), (3, 2), (2, 2)),
)
ORDER = tuple((half, block) for batch in BATCHES for half in (0, 1) for block in batch)


def slot_in_batch(half, first, second):
    slot = jnp.int32(0)
    for batch in BATCHES:
        for index, (du, dv) in enumerate(batch):
            here = (first == du) & (second == dv)
            slot = jnp.where(here, index + half * len(batch), slot)
    return slot


def kernel(
    route_hbm, pick_hbm, score_hbm, hidden_hbm, weight_hbm, out_ref,
    route, pick, score, hidden, weight, blocks, table, table_in, words, words_in, chooser,
    load_sem, gather_send, gather_recv, table_send, table_recv, word_send, word_recv, own_sem,
):
    g = lax.axis_index("group")
    m = lax.axis_index("member")
    z, core = g // 2, g % 2
    y, x = m // 4, m % 4

    loads = [
        pltpu.make_async_copy(source, target, load_sem.at[i])
        for i, (source, target) in enumerate(
            (
                (hidden_hbm, hidden),
                (route_hbm, route),
                (pick_hbm, pick),
                (score_hbm, score),
                (weight_hbm.at[:, pl.ds(0, 224), :], weight.at[:, pl.ds(0, 224), :]),
                (weight_hbm.at[:, pl.ds(224, 224), :], weight.at[:, pl.ds(256, 224), :]),
            )
        )
    ]
    for load in loads:
        load.start()

    def member_at(dx, dy):
        return ((y + dy) % 4) * 4 + (x + dx) % 4

    barrier = pltpu.get_barrier_semaphore()
    for dx, dy in ((1, 0), (3, 0), (0, 1), (0, 3)):
        pl.semaphore_signal(barrier, inc=1, device_id=(g, member_at(dx, dy)), device_id_type=MESH)

    def greet(i, carry):
        pl.semaphore_signal(barrier, inc=1, device_id=((g + i) % NG, m), device_id_type=MESH)
        return carry

    lax.fori_loop(1, NG, greet, 0)

    loads[0].wait()
    for half in (0, 1):
        at = 10 * half
        mine = half * NM + m
        blocks[mine, :, 0:4096] = hidden[at : at + 8, :]
        blocks[mine, :, 4096:WIDE] = jnp.concatenate(
            [hidden[at + 8 : at + 10, q * 1024 : (q + 1) * 1024] for q in range(4)], axis=0
        )

    pl.semaphore_wait(barrier, 4 + NG - 1)

    def offsets(half, du, dv):
        return (du, dv) if half == 0 else (dv, du)

    def slot_of(half, du, dv):
        dx, dy = offsets(half, du, dv)
        return half * NM + member_at(dx, dy)

    def part_of(slot, part):
        if part is None:
            return blocks.at[slot]
        return blocks.at[slot, :, pl.ds(part * HALF, HALF)]

    def copy(half, du, dv, part, su, sv):
        slot = slot_of(half, du, dv)
        ref = part_of(slot, part)
        index = ((half * 4 + (du - su) % 4) * 4 + (dv - sv) % 4) * 2 + (part or 0)
        return pltpu.make_async_remote_copy(
            src_ref=ref,
            dst_ref=ref,
            send_sem=gather_send,
            recv_sem=gather_recv.at[index],
            device_id=(g, member_at(*offsets(half, su, sv))),
            device_id_type=MESH,
        )

    def send(half, du, dv, part, su, sv):
        copy(half, du, dv, part, su, sv).start()

    def arrived(half, du, dv):
        parts = (0, 1) if 2 in (du, dv) and (dv == 2 or dv == 0) else (None,)
        for part in parts:
            slot = slot_of(half, du, dv)
            ref = part_of(slot, part)
            index = ((half * 4 + du) * 4 + dv) * 2 + (part or 0)
            pltpu.make_async_remote_copy(
                src_ref=ref, dst_ref=ref, send_sem=gather_send, recv_sem=gather_recv.at[index],
                device_id=(g, m), device_id_type=MESH,
            ).wait_recv()

    for half in (0, 1):
        send(half, 0, 0, None, 1, 0)
        send(half, 0, 0, None, 3, 0)
    for half in (0, 1):
        send(half, 0, 0, None, 0, 1)
        send(half, 0, 0, None, 0, 3)

    for load in loads[1:4]:
        load.wait()
    group_row = lax.broadcasted_iota(jnp.int32, (NG, 64), 0)
    chosen = [route[k : k + 1, :] == group_row for k in range(4)]
    per_token = sum(c.astype(jnp.float32) for c in chosen)
    before = (
        lax.broadcasted_iota(jnp.int32, (64, 64), 0) < lax.broadcasted_iota(jnp.int32, (64, 64), 1)
    ).astype(jnp.bfloat16)
    earlier = jnp.dot(per_token.astype(jnp.bfloat16), before, preferred_element_type=jnp.float32)
    ranks = [jnp.sum(jnp.where(c, earlier, 0.0), axis=0, keepdims=True) for c in chosen]
    routes = [route[k : k + 1, :].astype(jnp.float32) for k in range(4)]
    turned = jnp.transpose(jnp.concatenate(ranks + routes, axis=0), (1, 0))

    lane = lax.broadcasted_iota(jnp.int32, (1, LANES), 1)
    dx, dy = (z % 4 - x + 4) % 4, (z // 4 - y + 4) % 4
    slot = slot_in_batch(core, jnp.where(core == 0, dx, dy), jnp.where(core == 0, dy, dx))
    inner = lane % 8
    rank_of_lane = jnp.where(
        lane // 8 == slot, inner, jnp.where(lane // 8 == slot + 8, 8 + inner % 2, -1)
    ).astype(jnp.float32)
    total = jnp.zeros((NG, 2 * LANES), jnp.float32)
    for k in range(4):
        hit = (turned[:, k : k + 1] == rank_of_lane).astype(jnp.float32)
        both = []
        for e in range(2):
            coef = score[k, e : e + 1, :] * pick[k, e : e + 1, :].astype(jnp.float32)
            both.append(
                jnp.dot(
                    jnp.where(chosen[k], coef, 0.0), hit,
                    preferred_element_type=jnp.float32, precision=lax.Precision.HIGHEST,
                )
            )
        total = total + jnp.concatenate(both, axis=1)
    table[...] = total.reshape(NG, 1, 2 * LANES)

    def send_table(i, carry):
        to = (g + i) % NG
        pltpu.make_async_remote_copy(
            src_ref=table.at[to], dst_ref=table_in.at[g], send_sem=table_send, recv_sem=table_recv,
            device_id=(to, m), device_id_type=MESH,
        ).start()
        return carry

    lax.fori_loop(1, NG, send_table, 0)
    table_in[g] = table[g]

    row = lax.broadcasted_iota(jnp.int32, (1, 20 * NG), 1)
    piece, inside = (row % 20) // 4, row % 4
    segment = jnp.where(piece == 4, inside // 2, piece // 2)
    rank = jnp.where(piece == 4, 8 + inside % 2, (piece % 2) * 4 + inside)
    key = (10 * (row // 20) + rank).astype(jnp.float32)
    picks = jnp.zeros((64, 20 * NG), jnp.float32)
    for k in range(4):
        token_key = 10.0 * turned[:, 4 + k : 5 + k] + turned[:, k : k + 1]
        picks = picks + (token_key == key).astype(jnp.float32)
    for s in (0, 1):
        chooser[64 * s : 64 * (s + 1), :] = jnp.where(segment == s, picks, 0.0).astype(jnp.bfloat16)

    loads[4].wait()
    loads[5].wait()
    weight[:, 224:256, :] = jnp.zeros((2, 32, 2048), jnp.bfloat16)
    weight[:, 480:512, :] = jnp.zeros((2, 32, 2048), jnp.bfloat16)

    def multiply(batch, first_word):
        todo = [(half, du, dv) for half in (0, 1) for du, dv in batch]
        count = len(todo)
        slots = [slot_of(*block) for block in todo]
        padded = slots + [slots[0]] * (8 - count)
        coefs = None
        for half, du, dv in todo:
            home = 2 * member_at(*offsets(half, du, dv)) + half
            coefs = table_in[home] if coefs is None else coefs + table_in[home]
        each = []
        for q in range(4):
            part = coefs[:, (q // 2) * LANES : (q // 2 + 1) * LANES]
            each.append(jnp.where((lane < MAIN) | (inner // 2 == q), part, 0.0))
        columns = jnp.transpose(jnp.concatenate(each + each, axis=0), (1, 0))
        rest = [blocks[s, :, 4096:WIDE] for s in padded]
        result = None
        for q in range(4):
            left = jnp.concatenate(
                [blocks[s, :, q * 1024 : (q + 1) * 1024] for s in padded] + rest, axis=0
            )
            product = lax.dot_general(
                left, weight[q // 2, :, (q % 2) * 1024 : (q % 2 + 1) * 1024],
                (((1,), (1,)), ((), ())), preferred_element_type=jnp.float32,
            )
            product = product * columns[:, q : q + 1]
            result = product if result is None else result + product
        main = result[0 : 8 * count]
        tail = result[MAIN : MAIN + 8 * count]
        tail = tail + pltpu.roll(tail, 8 * count - 4, 0)
        tail = tail + pltpu.roll(tail, 8 * count - 2, 0)
        for rows, is_tail in ((main, False), (tail, True)):
            for s in (0, 1):
                values = rows[:, 256 * s : 256 * (s + 1)]
                peak = jnp.max(jnp.abs(values), axis=1, keepdims=True)
                power = jnp.ceil(jnp.log2(jnp.maximum(peak, 1e-30) * (1.0 / 32767.0)))
                fixed = values * jnp.exp2(-power)
                fixed = jnp.clip(jnp.round(fixed), -32767.0, 32767.0).astype(jnp.int32)
                high = jnp.where(lane < 96, fixed[:, LANES:], power.astype(jnp.int32))
                packed = (high << 16) | (fixed[:, :LANES] & 0xFFFF)
                for j in range(count):
                    if is_tail:
                        words[first_word + j, 4, 2 * s : 2 * s + 2, :] = packed[8 * j : 8 * j + 2]
                    else:
                        words[first_word + j, 2 * s] = packed[8 * j : 8 * j + 4]
                        words[first_word + j, 2 * s + 1] = packed[8 * j + 4 : 8 * j + 8]
        for j, (half, du, dv) in enumerate(todo):
            home = 2 * member_at(*offsets(half, du, dv)) + half

            @pl.when(home != g)
            def _():
                pltpu.make_async_remote_copy(
                    src_ref=words.at[first_word + j], dst_ref=words_in.at[g],
                    send_sem=word_send, recv_sem=word_recv,
                    device_id=(home, m), device_id_type=MESH,
                ).start()

            @pl.when(home == g)
            def _():
                pltpu.make_async_copy(words.at[first_word + j], words_in.at[g], own_sem).start()

        return first_word + count

    def both(step):
        for half in (0, 1):
            step(half)

    def near_first(half):
        arrived(half, 1, 0)
        arrived(half, 3, 0)
        send(half, 3, 0, 0, 1, 0)
        send(half, 1, 0, 1, 3, 0)
        for du in (1, 3):
            for sv in (1, 3):
                send(half, du, 0, None, 0, sv)

    def across(half, du):
        arrived(half, du, 1)
        arrived(half, du, 3)
        send(half, du, 3, 0, 0, 1)
        send(half, du, 1, 1, 0, 3)

    def far_first(half):
        arrived(half, 2, 0)
        for sv in (1, 3):
            send(half, 2, 0, None, 0, sv)

    def opposite(half, dus):
        for du in dus:
            arrived(half, du, 2)

    both(near_first)
    pltpu.make_async_remote_copy(
        src_ref=table.at[pl.ds(0, NG - 1)], dst_ref=table_in.at[pl.ds(0, NG - 1)],
        send_sem=table_send, recv_sem=table_recv, device_id=(g, m), device_id_type=MESH,
    ).wait()
    next_word = multiply(BATCHES[0], 0)
    both(far_first)
    both(lambda half: across(half, 0))
    next_word = multiply(BATCHES[1], next_word)
    both(lambda half: across(half, 1))
    both(lambda half: across(half, 3))
    next_word = multiply(BATCHES[2], next_word)
    both(lambda half: across(half, 2))
    both(lambda half: opposite(half, (0,)))
    next_word = multiply(BATCHES[3], next_word)
    both(lambda half: opposite(half, (1, 3, 2)))
    multiply(BATCHES[4], next_word)

    pltpu.make_async_remote_copy(
        src_ref=blocks.at[pl.ds(0, 30)], dst_ref=blocks.at[pl.ds(0, 30)],
        send_sem=gather_send, recv_sem=gather_recv.at[0], device_id=(g, m), device_id_type=MESH,
    ).wait_send()
    pltpu.make_async_copy(words.at[0], words_in.at[0], own_sem).wait()
    pltpu.make_async_remote_copy(
        src_ref=words.at[pl.ds(0, NG - 1)], dst_ref=words_in.at[pl.ds(0, NG - 1)],
        send_sem=word_send, recv_sem=word_recv, device_id=(g, m), device_id_type=MESH,
    ).wait()

    received = words_in[...].reshape(20 * NG, LANES)
    high = received >> 16
    low = (received << 16) >> 16
    scale = jnp.exp2(high[:, 96:97].astype(jnp.float32))
    values = jnp.concatenate([low, high], axis=1).astype(jnp.float32) * scale
    coarse = values.astype(jnp.bfloat16)
    fine = (values - coarse.astype(jnp.float32)).astype(jnp.bfloat16)
    taken = jnp.dot(chooser[...], coarse, preferred_element_type=jnp.float32)
    taken = taken + jnp.dot(chooser[...], fine, preferred_element_type=jnp.float32)
    out_ref[:, 0:224] = taken[0:64, 0:224].astype(jnp.bfloat16)
    out_ref[:, 224:448] = taken[64:128, 0:224].astype(jnp.bfloat16)


def per_device(route_group, expert_pick, route_score, expert_hidden, down_weight):
    any_spec = pl.BlockSpec(memory_space=pl.ANY)
    return pl.pallas_call(
        kernel,
        out_shape=jax.ShapeDtypeStruct((64, 448), jnp.bfloat16),
        in_specs=[any_spec] * 5,
        out_specs=pl.BlockSpec(memory_space=pltpu.VMEM),
        scratch_shapes=[
            pltpu.VMEM((4, 64), jnp.int32),
            pltpu.VMEM((4, 2, 64), jnp.int32),
            pltpu.VMEM((4, 2, 64), jnp.float32),
            pltpu.VMEM((20, 4096), jnp.bfloat16),
            pltpu.VMEM((2, 512, 2048), jnp.bfloat16),
            pltpu.VMEM((2 * NM, ROWS, WIDE), jnp.bfloat16),
            pltpu.VMEM((NG, 1, 2 * LANES), jnp.float32),
            pltpu.VMEM((NG, 1, 2 * LANES), jnp.float32),
            pltpu.VMEM((NG, 5, 4, LANES), jnp.int32),
            pltpu.VMEM((NG, 5, 4, LANES), jnp.int32),
            pltpu.VMEM((LANES, 20 * NG), jnp.bfloat16),
            pltpu.SemaphoreType.DMA((6,)),
            pltpu.SemaphoreType.DMA,
            pltpu.SemaphoreType.DMA((64,)),
            pltpu.SemaphoreType.DMA,
            pltpu.SemaphoreType.DMA,
            pltpu.SemaphoreType.DMA,
            pltpu.SemaphoreType.DMA,
            pltpu.SemaphoreType.DMA,
        ],
        compiler_params=pltpu.CompilerParams(
            collective_id=0, has_side_effects=True, vmem_limit_bytes=40 << 20
        ),
        name="experts_return",
    )(
        jnp.transpose(route_group, (1, 0)),
        jnp.transpose(expert_pick, (1, 2, 0)),
        jnp.transpose(route_score, (1, 2, 0)),
        expert_hidden[0],
        jnp.swapaxes(down_weight[0], 1, 2),
    )


def solution(mesh):
    placed = (
        P("group", None),
        P("group", None, None),
        P("group", None, None),
        P("group", "member", None),
        P("group", None, None, "member"),
    )
    return jax.shard_map(
        per_device, mesh=mesh, in_specs=placed, out_specs=P("group", "member"), check_vma=False
    )
```

```python
import functools

import jax
import jax.numpy as jnp
from jax import lax
from jax.experimental import pallas as pl
from jax.experimental.pallas import tpu as pltpu
from jax.sharding import PartitionSpec as P

MESH = pl.DeviceIdType.MESH
NG = 32
NM = 16
ROWS = 8
WIDE = 5120
HALF = WIDE // 2
LANES = 128
MAIN = 64

BATCHES = (
    ((0, 0), (1, 0), (3, 0)),
    ((2, 0), (0, 1), (0, 3)),
    ((1, 1), (3, 1), (1, 3), (3, 3)),
    ((2, 1), (2, 3), (0, 2)),
    ((3, 2), (1, 2)),
    ((2, 2),),
)


def slot_in_batch(half, first, second):
    slot = jnp.int32(0)
    for batch in BATCHES:
        for index, (du, dv) in enumerate(batch):
            here = (first == du) & (second == dv)
            slot = jnp.where(here, index + half * len(batch), slot)
    return slot


def kernel(
    route_hbm, pick_hbm, score_hbm, hidden_hbm, weight_hbm, out_ref,
    route, pick, score, hidden, weight, blocks, table, table_in, products, words, words_in, chooser,
    load_sem, gather_send, gather_recv, table_send, table_recv, word_send, word_recv, own_sem,
):
    g = lax.axis_index("group")
    m = lax.axis_index("member")
    z, core = g // 2, g % 2
    y, x = m // 4, m % 4

    loads = [
        pltpu.make_async_copy(source, target, load_sem.at[i])
        for i, (source, target) in enumerate(
            (
                (hidden_hbm, hidden),
                (route_hbm, route),
                (pick_hbm, pick),
                (score_hbm, score),
                (weight_hbm.at[:, pl.ds(0, 224), :], weight.at[:, pl.ds(0, 224), :]),
                (weight_hbm.at[:, pl.ds(224, 224), :], weight.at[:, pl.ds(256, 224), :]),
            )
        )
    ]
    for load in loads:
        load.start()

    def member_at(dx, dy):
        return ((y + dy) % 4) * 4 + (x + dx) % 4

    barrier = pltpu.get_barrier_semaphore()
    for dx, dy in ((1, 0), (3, 0), (0, 1), (0, 3)):
        pl.semaphore_signal(barrier, inc=1, device_id=(g, member_at(dx, dy)), device_id_type=MESH)

    far_first = [sign * steps for steps in range(NG // 2, 0, -1) for sign in (1, -1)][1:]
    for steps in far_first:
        pl.semaphore_signal(barrier, inc=1, device_id=((g + steps) % NG, m), device_id_type=MESH)

    loads[0].wait()
    for half in (0, 1):
        at = 10 * half
        mine = half * NM + m
        blocks[mine, :, 0:4096] = hidden[at : at + 8, :]
        blocks[mine, :, 4096:WIDE] = jnp.concatenate(
            [hidden[at + 8 : at + 10, q * 1024 : (q + 1) * 1024] for q in range(4)], axis=0
        )

    for load in loads[1:4]:
        load.wait()
    group_row = lax.broadcasted_iota(jnp.int32, (NG, 64), 0)
    chosen = [route[k : k + 1, :] == group_row for k in range(4)]
    per_token = sum(c.astype(jnp.float32) for c in chosen)
    before = (
        lax.broadcasted_iota(jnp.int32, (64, 64), 0) < lax.broadcasted_iota(jnp.int32, (64, 64), 1)
    ).astype(jnp.bfloat16)
    earlier = jnp.dot(per_token.astype(jnp.bfloat16), before, preferred_element_type=jnp.float32)
    ranks = [jnp.sum(jnp.where(c, earlier, 0.0), axis=0, keepdims=True) for c in chosen]
    routes = [route[k : k + 1, :].astype(jnp.float32) for k in range(4)]
    turned = jnp.transpose(jnp.concatenate(ranks + routes, axis=0), (1, 0))

    lane = lax.broadcasted_iota(jnp.int32, (1, LANES), 1)
    dx, dy = (z % 4 - x + 4) % 4, (z // 4 - y + 4) % 4
    slot = slot_in_batch(core, jnp.where(core == 0, dx, dy), jnp.where(core == 0, dy, dx))
    inner = lane % 8
    rank_of_lane = jnp.where(
        lane // 8 == slot, inner, jnp.where(lane // 8 == slot + 8, 8 + inner % 2, -1)
    ).astype(jnp.float32)
    total = jnp.zeros((NG, 2 * LANES), jnp.float32)
    for k in range(4):
        hit = (turned[:, k : k + 1] == rank_of_lane).astype(jnp.float32)
        both = []
        for e in range(2):
            coef = score[k, e : e + 1, :] * pick[k, e : e + 1, :].astype(jnp.float32)
            both.append(
                jnp.dot(
                    jnp.where(chosen[k], coef, 0.0), hit,
                    preferred_element_type=jnp.float32, precision=lax.Precision.HIGHEST,
                )
            )
        total = total + jnp.concatenate(both, axis=1)
    table[...] = total.reshape(NG, 1, 2 * LANES)

    pl.semaphore_wait(barrier, 4 + NG - 1)

    def offsets(half, du, dv):
        return (du, dv) if half == 0 else (dv, du)

    def slot_of(half, du, dv):
        dx, dy = offsets(half, du, dv)
        return half * NM + member_at(dx, dy)

    def part_of(slot, part):
        return blocks.at[slot, :, pl.ds(part * HALF, HALF)]

    def copy(half, du, dv, part, su, sv):
        slot = slot_of(half, du, dv)
        ref = part_of(slot, part)
        index = ((half * 4 + (du - su) % 4) * 4 + (dv - sv) % 4) * 2 + part
        return pltpu.make_async_remote_copy(
            src_ref=ref,
            dst_ref=ref,
            send_sem=gather_send,
            recv_sem=gather_recv.at[index],
            device_id=(g, member_at(*offsets(half, su, sv))),
            device_id_type=MESH,
        )

    def send(half, du, dv, part, su, sv):
        copy(half, du, dv, part, su, sv).start()

    def arrived(half, du, dv, part):
        ref = part_of(slot_of(half, du, dv), part)
        index = ((half * 4 + du) * 4 + dv) * 2 + part
        pltpu.make_async_remote_copy(
            src_ref=ref, dst_ref=ref, send_sem=gather_send, recv_sem=gather_recv.at[index],
            device_id=(g, m), device_id_type=MESH,
        ).wait_recv()

    along = ((1, 0), (3, 0))
    cross = ((0, 1), (0, 3))

    def spread(half, du, dv, parts, targets):
        for part, (su, sv) in zip(parts, targets):
            send(half, du, dv, part, su, sv)

    for parts in ((0, 1), (1, 0)):
        for half in (0, 1):
            spread(half, 0, 0, parts, along)
    for steps in far_first:
        to = (g + steps) % NG
        pltpu.make_async_remote_copy(
            src_ref=table.at[to], dst_ref=table_in.at[g], send_sem=table_send, recv_sem=table_recv,
            device_id=(to, m), device_id_type=MESH,
        ).start()
    table_in[g] = table[g]

    for parts in ((0, 1), (1, 0)):
        for half in (0, 1):
            spread(half, 0, 0, parts, cross)

    row = lax.broadcasted_iota(jnp.int32, (1, 20 * NG), 1)
    piece, inside = (row % 20) // 4, row % 4
    segment = jnp.where(piece == 4, inside // 2, piece // 2)
    rank = jnp.where(piece == 4, 8 + inside % 2, (piece % 2) * 4 + inside)
    key = (10 * (row // 20) + rank).astype(jnp.float32)
    picks = jnp.zeros((64, 20 * NG), jnp.float32)
    for k in range(4):
        token_key = 10.0 * turned[:, 4 + k : 5 + k] + turned[:, k : k + 1]
        picks = picks + (token_key == key).astype(jnp.float32)
    for s in (0, 1):
        chooser[64 * s : 64 * (s + 1), :] = jnp.where(segment == s, picks, 0.0).astype(jnp.bfloat16)

    loads[4].wait()
    loads[5].wait()
    weight[:, 224:256, :] = jnp.zeros((2, 32, 2048), jnp.bfloat16)
    weight[:, 480:512, :] = jnp.zeros((2, 32, 2048), jnp.bfloat16)

    def blocks_of(batch):
        return [(half, du, dv) for half in (0, 1) for du, dv in batch]

    def multiply(number):
        slots = [slot_of(*block) for block in blocks_of(BATCHES[number])]
        rows = 8 * len(slots)
        rest = [blocks[s, :, 4096:WIDE] for s in slots]
        line = lax.broadcasted_iota(jnp.int32, (2 * rows, 1), 0)
        for e in range(2):
            result = None
            for q in (2 * e, 2 * e + 1):
                left = jnp.concatenate(
                    [blocks[s, :, q * 1024 : (q + 1) * 1024] for s in slots] + rest, axis=0
                )
                product = lax.dot_general(
                    left, weight[e, :, (q % 2) * 1024 : (q % 2 + 1) * 1024],
                    (((1,), (1,)), ((), ())), preferred_element_type=jnp.float32,
                )
                product = jnp.where((line < rows) | ((line % 8) // 2 == q), product, 0.0)
                result = product if result is None else result + product
            products[number, e, 0:rows] = result[:rows]
            products[number, e, MAIN : MAIN + rows] = result[rows:]

    def finish(number):
        todo = blocks_of(BATCHES[number])
        count = len(todo)
        first_word = sum(2 * len(batch) for batch in BATCHES[:number])
        coefs = None
        for half, du, dv in todo:
            home = 2 * member_at(*offsets(half, du, dv)) + half
            coefs = table_in[home] if coefs is None else coefs + table_in[home]
        rows = [coefs[:, :LANES], coefs[:, LANES:]] * 4
        columns = jnp.transpose(jnp.concatenate(rows, axis=0), (1, 0))

        def weighted(at):
            rows = slice(at, at + 8 * count)
            first = products[number, 0, rows] * columns[rows, 0:1]
            return first + products[number, 1, rows] * columns[rows, 1:2]

        main, tail = weighted(0), weighted(MAIN)
        tail = tail + pltpu.roll(tail, 8 * count - 4, 0)
        tail = tail + pltpu.roll(tail, 8 * count - 2, 0)
        for rows, is_tail in ((main, False), (tail, True)):
            for s in (0, 1):
                values = rows[:, 256 * s : 256 * (s + 1)]
                peak = jnp.max(jnp.abs(values), axis=1, keepdims=True)
                power = jnp.ceil(jnp.log2(jnp.maximum(peak, 1e-30) * (1.0 / 32767.0)))
                fixed = values * jnp.exp2(-power)
                fixed = jnp.clip(jnp.round(fixed), -32767.0, 32767.0).astype(jnp.int32)
                high = jnp.where(lane < 96, fixed[:, LANES:], power.astype(jnp.int32))
                packed = (high << 16) | (fixed[:, :LANES] & 0xFFFF)
                for j in range(count):
                    if is_tail:
                        words[first_word + j, 4, 2 * s : 2 * s + 2, :] = packed[8 * j : 8 * j + 2]
                    else:
                        words[first_word + j, 2 * s] = packed[8 * j : 8 * j + 4]
                        words[first_word + j, 2 * s + 1] = packed[8 * j + 4 : 8 * j + 8]
        for j, (half, du, dv) in enumerate(todo):
            home = 2 * member_at(*offsets(half, du, dv)) + half

            @pl.when(home != g)
            def _():
                pltpu.make_async_remote_copy(
                    src_ref=words.at[first_word + j], dst_ref=words_in.at[g],
                    send_sem=word_send, recv_sem=word_recv,
                    device_id=(home, m), device_id_type=MESH,
                ).start()

            @pl.when(home == g)
            def _():
                pltpu.make_async_copy(words.at[first_word + j], words_in.at[g], own_sem).start()

    def pass_along(half):
        arrived(half, 3, 0, 0)
        arrived(half, 1, 0, 1)
        send(half, 3, 0, 0, 1, 0)
        send(half, 1, 0, 1, 3, 0)

    def pass_cross(half, du):
        arrived(half, du, 3, 0)
        arrived(half, du, 1, 1)
        send(half, du, 3, 0, 0, 1)
        send(half, du, 1, 1, 0, 3)

    def rest_cross(half, du):
        arrived(half, du, 3, 1)
        arrived(half, du, 1, 0)

    def opposite(half, du):
        arrived(half, du, 2, 0)
        arrived(half, du, 2, 1)

    halves = (0, 1)
    for half in halves:
        pass_along(half)
    for half in halves:
        spread(half, 3, 0, (0, 0), cross)
        spread(half, 1, 0, (1, 1), cross[::-1])
    for half in halves:
        arrived(half, 3, 0, 1)
        arrived(half, 1, 0, 0)
        spread(half, 3, 0, (1, 1), cross[::-1])
        spread(half, 1, 0, (0, 0), cross)
    multiply(0)
    for half in halves:
        pass_cross(half, 0)
    for half in halves:
        arrived(half, 2, 0, 0)
        arrived(half, 2, 0, 1)
        spread(half, 2, 0, (0, 1), cross)
        spread(half, 2, 0, (1, 0), cross)
    for du in (0,):
        for half in halves:
            rest_cross(half, du)
    multiply(1)
    for du in (3, 1):
        for half in halves:
            pass_cross(half, du)
    tables = pltpu.make_async_remote_copy(
        src_ref=table.at[pl.ds(0, NG - 1)], dst_ref=table_in.at[pl.ds(0, NG - 1)],
        send_sem=table_send, recv_sem=table_recv, device_id=(g, m), device_id_type=MESH,
    )
    tables.wait_recv()
    finish(0)
    finish(1)
    for du in (3, 1):
        for half in halves:
            rest_cross(half, du)
    multiply(2)
    finish(2)
    for half in halves:
        pass_cross(half, 2)
    for du in (2,):
        for half in halves:
            rest_cross(half, du)
    for du in (0,):
        for half in halves:
            opposite(half, du)
    multiply(3)
    finish(3)
    for du in (3, 1):
        for half in halves:
            opposite(half, du)
    multiply(4)
    finish(4)
    for du in (2,):
        for half in halves:
            opposite(half, du)
    multiply(5)
    finish(5)
    tables.wait_send()

    pltpu.make_async_remote_copy(
        src_ref=blocks.at[pl.ds(0, 30)], dst_ref=blocks.at[pl.ds(0, 30)],
        send_sem=gather_send, recv_sem=gather_recv.at[0], device_id=(g, m), device_id_type=MESH,
    ).wait_send()
    pltpu.make_async_copy(words.at[0], words_in.at[0], own_sem).wait()
    pltpu.make_async_remote_copy(
        src_ref=words.at[pl.ds(0, NG - 1)], dst_ref=words_in.at[pl.ds(0, NG - 1)],
        send_sem=word_send, recv_sem=word_recv, device_id=(g, m), device_id_type=MESH,
    ).wait()

    received = words_in[...].reshape(20 * NG, LANES)
    high = received >> 16
    low = (received << 16) >> 16
    scale = jnp.exp2(high[:, 96:97].astype(jnp.float32))
    values = jnp.concatenate([low, high], axis=1).astype(jnp.float32) * scale
    coarse = values.astype(jnp.bfloat16)
    fine = (values - coarse.astype(jnp.float32)).astype(jnp.bfloat16)
    taken = jnp.dot(chooser[...], coarse, preferred_element_type=jnp.float32)
    taken = taken + jnp.dot(chooser[...], fine, preferred_element_type=jnp.float32)
    out_ref[:, 0:224] = taken[0:64, 0:224].astype(jnp.bfloat16)
    out_ref[:, 224:448] = taken[64:128, 0:224].astype(jnp.bfloat16)


def per_device(route_group, expert_pick, route_score, expert_hidden, down_weight):
    hbm = pl.BlockSpec(memory_space=pl.ANY)
    return pl.pallas_call(
        kernel,
        out_shape=jax.ShapeDtypeStruct((64, 448), jnp.bfloat16),
        in_specs=[hbm] * 5,
        out_specs=pl.BlockSpec(memory_space=pltpu.VMEM),
        scratch_shapes=[
            pltpu.VMEM((4, 64), jnp.int32),
            pltpu.VMEM((4, 2, 64), jnp.int32),
            pltpu.VMEM((4, 2, 64), jnp.float32),
            pltpu.VMEM((20, 4096), jnp.bfloat16),
            pltpu.VMEM((2, 512, 2048), jnp.bfloat16),
            pltpu.VMEM((2 * NM, ROWS, WIDE), jnp.bfloat16),
            pltpu.VMEM((NG, 1, 2 * LANES), jnp.float32),
            pltpu.VMEM((NG, 1, 2 * LANES), jnp.float32),
            pltpu.VMEM((len(BATCHES), 2, LANES, 512), jnp.float32),
            pltpu.VMEM((NG, 5, 4, LANES), jnp.int32),
            pltpu.VMEM((NG, 5, 4, LANES), jnp.int32),
            pltpu.VMEM((LANES, 20 * NG), jnp.bfloat16),
            pltpu.SemaphoreType.DMA((6,)),
            pltpu.SemaphoreType.DMA,
            pltpu.SemaphoreType.DMA((64,)),
            pltpu.SemaphoreType.DMA,
            pltpu.SemaphoreType.DMA,
            pltpu.SemaphoreType.DMA,
            pltpu.SemaphoreType.DMA,
            pltpu.SemaphoreType.DMA,
        ],
        compiler_params=pltpu.CompilerParams(
            collective_id=0, has_side_effects=True, vmem_limit_bytes=63 << 20
        ),
        name="experts_return",
    )(
        jnp.transpose(route_group, (1, 0)),
        jnp.transpose(expert_pick, (1, 2, 0)),
        jnp.transpose(route_score, (1, 2, 0)),
        expert_hidden[0],
        jnp.swapaxes(down_weight[0], 1, 2),
    )


def solution(mesh):
    placed = (
        P("group", None),
        P("group", None, None),
        P("group", None, None),
        P("group", "member", None),
        P("group", None, None, "member"),
    )
    return jax.shard_map(
        per_device, mesh=mesh, in_specs=placed, out_specs=P("group", "member"), check_vma=False
    )
```

```python
import functools

import jax
import jax.numpy as jnp
from jax import lax
from jax.experimental import pallas as pl
from jax.experimental.pallas import tpu as pltpu
from jax.sharding import PartitionSpec as P

MESH = pl.DeviceIdType.MESH
NG = 32
NM = 16
ROWS = 8
WIDE = 5120
HALF = WIDE // 2
LANES = 128
MAIN = 64

BATCHES = (
    ((0, 0), (1, 0), (3, 0)),
    ((2, 0), (0, 1), (0, 3)),
    ((1, 1), (3, 1), (1, 3), (3, 3)),
    ((2, 1), (2, 3), (0, 2)),
    ((3, 2), (1, 2)),
    ((2, 2),),
)


def slot_in_batch(half, first, second):
    slot = jnp.int32(0)
    for batch in BATCHES:
        for index, (du, dv) in enumerate(batch):
            here = (first == du) & (second == dv)
            slot = jnp.where(here, index + half * len(batch), slot)
    return slot


def kernel(
    route_hbm, pick_hbm, score_hbm, hidden_hbm, weight_hbm, out_ref,
    route, pick, score, hidden, weight, blocks, table, table_in, products, words, words_in, chooser,
    load_sem, gather_send, gather_recv, table_send, table_recv, word_send, word_recv, own_sem,
    round_sem,
):
    g = lax.axis_index("group")
    m = lax.axis_index("member")
    z, core = g // 2, g % 2
    y, x = m // 4, m % 4

    loads = [
        pltpu.make_async_copy(source, target, load_sem.at[i])
        for i, (source, target) in enumerate(
            (
                (hidden_hbm, hidden),
                (route_hbm, route),
                (pick_hbm, pick),
                (score_hbm, score),
                (weight_hbm.at[:, pl.ds(0, 224), :], weight.at[:, pl.ds(0, 224), :]),
                (weight_hbm.at[:, pl.ds(224, 224), :], weight.at[:, pl.ds(256, 224), :]),
            )
        )
    ]
    for load in loads:
        load.start()

    def member_at(dx, dy):
        return ((y + dy) % 4) * 4 + (x + dx) % 4

    barrier = pltpu.get_barrier_semaphore()
    for dx, dy in ((1, 0), (3, 0), (0, 1), (0, 3)):
        pl.semaphore_signal(barrier, inc=1, device_id=(g, member_at(dx, dy)), device_id_type=MESH)

    def along_z(steps):
        return (g + 2 * steps) % NG

    other_core = g + 1 - 2 * core
    for to in [along_z(steps) for steps in (2, -2, 1, -1)] + [other_core]:
        pl.semaphore_signal(barrier, inc=1, device_id=(to, m), device_id_type=MESH)

    loads[0].wait()
    for half in (0, 1):
        at = 10 * half
        mine = half * NM + m
        blocks[mine, :, 0:4096] = hidden[at : at + 8, :]
        blocks[mine, :, 4096:WIDE] = jnp.concatenate(
            [hidden[at + 8 : at + 10, q * 1024 : (q + 1) * 1024] for q in range(4)], axis=0
        )

    pl.semaphore_wait(barrier, 9)

    def tell(step, targets):
        for to in targets:
            pl.semaphore_signal(round_sem.at[step], inc=1, device_id=(to, m), device_id_type=MESH)

    def told(step, count):
        pl.semaphore_wait(round_sem.at[step], count)

    tell(0, [along_z(steps) for steps in (2, -2, 1, -1)])

    def offsets(half, du, dv):
        return (du, dv) if half == 0 else (dv, du)

    def slot_of(half, du, dv):
        dx, dy = offsets(half, du, dv)
        return half * NM + member_at(dx, dy)

    def part_of(slot, part):
        return blocks.at[slot, :, pl.ds(part * HALF, HALF)]

    def copy(half, du, dv, part, su, sv):
        slot = slot_of(half, du, dv)
        ref = part_of(slot, part)
        index = ((half * 4 + (du - su) % 4) * 4 + (dv - sv) % 4) * 2 + part
        return pltpu.make_async_remote_copy(
            src_ref=ref,
            dst_ref=ref,
            send_sem=gather_send,
            recv_sem=gather_recv.at[index],
            device_id=(g, member_at(*offsets(half, su, sv))),
            device_id_type=MESH,
        )

    def send(half, du, dv, part, su, sv):
        copy(half, du, dv, part, su, sv).start()

    def arrived(half, du, dv, part):
        ref = part_of(slot_of(half, du, dv), part)
        index = ((half * 4 + du) * 4 + dv) * 2 + part
        pltpu.make_async_remote_copy(
            src_ref=ref, dst_ref=ref, send_sem=gather_send, recv_sem=gather_recv.at[index],
            device_id=(g, m), device_id_type=MESH,
        ).wait_recv()

    along = ((1, 0), (3, 0))
    cross = ((0, 1), (0, 3))

    def spread(half, du, dv, parts, targets):
        for part, (su, sv) in zip(parts, targets):
            send(half, du, dv, part, su, sv)

    for parts in ((0, 1), (1, 0)):
        for half in (0, 1):
            spread(half, 0, 0, parts, along)
    for parts in ((0, 1), (1, 0)):
        for half in (0, 1):
            spread(half, 0, 0, parts, cross)

    for load in loads[1:4]:
        load.wait()
    group_row = lax.broadcasted_iota(jnp.int32, (NG, 64), 0)
    chosen = [route[k : k + 1, :] == group_row for k in range(4)]
    per_token = sum(c.astype(jnp.float32) for c in chosen)
    before = (
        lax.broadcasted_iota(jnp.int32, (64, 64), 0) < lax.broadcasted_iota(jnp.int32, (64, 64), 1)
    ).astype(jnp.bfloat16)
    earlier = jnp.dot(per_token.astype(jnp.bfloat16), before, preferred_element_type=jnp.float32)
    ranks = [jnp.sum(jnp.where(c, earlier, 0.0), axis=0, keepdims=True) for c in chosen]
    routes = [route[k : k + 1, :].astype(jnp.float32) for k in range(4)]
    turned = jnp.transpose(jnp.concatenate(ranks + routes, axis=0), (1, 0))

    lane = lax.broadcasted_iota(jnp.int32, (1, LANES), 1)
    dx, dy = (z % 4 - x + 4) % 4, (z // 4 - y + 4) % 4
    slot = slot_in_batch(core, jnp.where(core == 0, dx, dy), jnp.where(core == 0, dy, dx))
    inner = lane % 8
    rank_of_lane = jnp.where(
        lane // 8 == slot, inner, jnp.where(lane // 8 == slot + 8, 8 + inner % 2, -1)
    ).astype(jnp.float32)
    total = jnp.zeros((NG, 2 * LANES), jnp.float32)
    for k in range(4):
        hit = (turned[:, k : k + 1] == rank_of_lane).astype(jnp.float32)
        both = []
        for e in range(2):
            coef = score[k, e : e + 1, :] * pick[k, e : e + 1, :].astype(jnp.float32)
            both.append(
                jnp.dot(
                    jnp.where(chosen[k], coef, 0.0), hit,
                    preferred_element_type=jnp.float32, precision=lax.Precision.HIGHEST,
                )
            )
        total = total + jnp.concatenate(both, axis=1)
    table[...] = total.reshape(NG, 1, 2 * LANES)

    told(0, 4)
    tell(1, [along_z(steps) for steps in (4, -4, 3, -3)])

    row = lax.broadcasted_iota(jnp.int32, (1, 20 * NG), 1)
    piece, inside = (row % 20) // 4, row % 4
    segment = jnp.where(piece == 4, inside // 2, piece // 2)
    rank = jnp.where(piece == 4, 8 + inside % 2, (piece % 2) * 4 + inside)
    key = (10 * (row // 20) + rank).astype(jnp.float32)
    picks = jnp.zeros((64, 20 * NG), jnp.float32)
    for k in range(4):
        token_key = 10.0 * turned[:, 4 + k : 5 + k] + turned[:, k : k + 1]
        picks = picks + (token_key == key).astype(jnp.float32)
    for s in (0, 1):
        chooser[64 * s : 64 * (s + 1), :] = jnp.where(segment == s, picks, 0.0).astype(jnp.bfloat16)

    loads[4].wait()
    loads[5].wait()
    weight[:, 224:256, :] = jnp.zeros((2, 32, 2048), jnp.bfloat16)
    weight[:, 480:512, :] = jnp.zeros((2, 32, 2048), jnp.bfloat16)

    def blocks_of(batch):
        return [(half, du, dv) for half in (0, 1) for du, dv in batch]

    def multiply(number):
        slots = [slot_of(*block) for block in blocks_of(BATCHES[number])]
        rows = 8 * len(slots)
        rest = [blocks[s, :, 4096:WIDE] for s in slots]
        line = lax.broadcasted_iota(jnp.int32, (2 * rows, 1), 0)
        for e in range(2):
            result = None
            for q in (2 * e, 2 * e + 1):
                left = jnp.concatenate(
                    [blocks[s, :, q * 1024 : (q + 1) * 1024] for s in slots] + rest, axis=0
                )
                product = lax.dot_general(
                    left, weight[e, :, (q % 2) * 1024 : (q % 2 + 1) * 1024],
                    (((1,), (1,)), ((), ())), preferred_element_type=jnp.float32,
                )
                product = jnp.where((line < rows) | ((line % 8) // 2 == q), product, 0.0)
                result = product if result is None else result + product
            products[number, e, 0:rows] = result[:rows]
            products[number, e, MAIN : MAIN + rows] = result[rows:]

    def finish(number):
        todo = blocks_of(BATCHES[number])
        count = len(todo)
        first_word = sum(2 * len(batch) for batch in BATCHES[:number])
        coefs = None
        for half, du, dv in todo:
            home = 2 * member_at(*offsets(half, du, dv)) + half
            coefs = table_in[home] if coefs is None else coefs + table_in[home]
        rows = [coefs[:, :LANES], coefs[:, LANES:]] * 4
        columns = jnp.transpose(jnp.concatenate(rows, axis=0), (1, 0))

        def weighted(at):
            rows = slice(at, at + 8 * count)
            first = products[number, 0, rows] * columns[rows, 0:1]
            return first + products[number, 1, rows] * columns[rows, 1:2]

        main, tail = weighted(0), weighted(MAIN)
        tail = tail + pltpu.roll(tail, 8 * count - 4, 0)
        tail = tail + pltpu.roll(tail, 8 * count - 2, 0)
        for rows, is_tail in ((main, False), (tail, True)):
            for s in (0, 1):
                values = rows[:, 256 * s : 256 * (s + 1)]
                peak = jnp.max(jnp.abs(values), axis=1, keepdims=True)
                power = jnp.ceil(jnp.log2(jnp.maximum(peak, 1e-30) * (1.0 / 32767.0)))
                fixed = values * jnp.exp2(-power)
                fixed = jnp.clip(jnp.round(fixed), -32767.0, 32767.0).astype(jnp.int32)
                high = jnp.where(lane < 96, fixed[:, LANES:], power.astype(jnp.int32))
                packed = (high << 16) | (fixed[:, :LANES] & 0xFFFF)
                for j in range(count):
                    if is_tail:
                        words[first_word + j, 4, 2 * s : 2 * s + 2, :] = packed[8 * j : 8 * j + 2]
                    else:
                        words[first_word + j, 2 * s] = packed[8 * j : 8 * j + 4]
                        words[first_word + j, 2 * s + 1] = packed[8 * j + 4 : 8 * j + 8]
        for j, (half, du, dv) in enumerate(todo):
            home = 2 * member_at(*offsets(half, du, dv)) + half

            @pl.when(home != g)
            def _():
                pltpu.make_async_remote_copy(
                    src_ref=words.at[first_word + j], dst_ref=words_in.at[g],
                    send_sem=word_send, recv_sem=word_recv,
                    device_id=(home, m), device_id_type=MESH,
                ).start()

            @pl.when(home == g)
            def _():
                pltpu.make_async_copy(words.at[first_word + j], words_in.at[g], own_sem).start()

    def pass_along(half):
        arrived(half, 3, 0, 0)
        arrived(half, 1, 0, 1)
        send(half, 3, 0, 0, 1, 0)
        send(half, 1, 0, 1, 3, 0)

    def pass_cross(half, du):
        arrived(half, du, 3, 0)
        arrived(half, du, 1, 1)
        send(half, du, 3, 0, 0, 1)
        send(half, du, 1, 1, 0, 3)

    def rest_cross(half, du):
        arrived(half, du, 3, 1)
        arrived(half, du, 1, 0)

    def opposite(half, du):
        arrived(half, du, 2, 0)
        arrived(half, du, 2, 1)

    halves = (0, 1)
    for half in halves:
        pass_along(half)
    for half in halves:
        spread(half, 3, 0, (0, 0), cross)
        spread(half, 1, 0, (1, 1), cross[::-1])
    for half in halves:
        arrived(half, 3, 0, 1)
        arrived(half, 1, 0, 0)
        spread(half, 3, 0, (1, 1), cross[::-1])
        spread(half, 1, 0, (0, 0), cross)
    told(1, 4)
    tell(2, [other_core])
    told(2, 1)
    for steps in [sign * steps for steps in range(NG // 2, 0, -1) for sign in (1, -1)][1:]:
        to = (g + steps) % NG
        pltpu.make_async_remote_copy(
            src_ref=table.at[to], dst_ref=table_in.at[g], send_sem=table_send, recv_sem=table_recv,
            device_id=(to, m), device_id_type=MESH,
        ).start()
    table_in[g] = table[g]
    for half in halves:
        pass_cross(half, 0)
    multiply(0)
    for half in halves:
        arrived(half, 2, 0, 0)
        arrived(half, 2, 0, 1)
        spread(half, 2, 0, (0, 1), cross)
        spread(half, 2, 0, (1, 0), cross)
    for du in (0,):
        for half in halves:
            rest_cross(half, du)
    multiply(1)
    for du in (3, 1):
        for half in halves:
            pass_cross(half, du)
    for du in (3, 1):
        for half in halves:
            rest_cross(half, du)
    multiply(2)
    for half in halves:
        pass_cross(half, 2)
    tables = pltpu.make_async_remote_copy(
        src_ref=table.at[pl.ds(0, NG - 1)], dst_ref=table_in.at[pl.ds(0, NG - 1)],
        send_sem=table_send, recv_sem=table_recv, device_id=(g, m), device_id_type=MESH,
    )
    tables.wait_recv()
    finish(0)
    finish(1)
    finish(2)
    for du in (2,):
        for half in halves:
            rest_cross(half, du)
    for du in (0,):
        for half in halves:
            opposite(half, du)
    multiply(3)
    finish(3)
    for du in (3, 1):
        for half in halves:
            opposite(half, du)
    multiply(4)
    finish(4)
    for du in (2,):
        for half in halves:
            opposite(half, du)
    multiply(5)
    finish(5)
    tables.wait_send()

    pltpu.make_async_remote_copy(
        src_ref=blocks.at[pl.ds(0, 30)], dst_ref=blocks.at[pl.ds(0, 30)],
        send_sem=gather_send, recv_sem=gather_recv.at[0], device_id=(g, m), device_id_type=MESH,
    ).wait_send()
    pltpu.make_async_copy(words.at[0], words_in.at[0], own_sem).wait()
    pltpu.make_async_remote_copy(
        src_ref=words.at[pl.ds(0, NG - 1)], dst_ref=words_in.at[pl.ds(0, NG - 1)],
        send_sem=word_send, recv_sem=word_recv, device_id=(g, m), device_id_type=MESH,
    ).wait()

    received = words_in[...].reshape(20 * NG, LANES)
    high = received >> 16
    low = (received << 16) >> 16
    scale = jnp.exp2(high[:, 96:97].astype(jnp.float32))
    values = jnp.concatenate([low, high], axis=1).astype(jnp.float32) * scale
    coarse = values.astype(jnp.bfloat16)
    fine = (values - coarse.astype(jnp.float32)).astype(jnp.bfloat16)
    taken = jnp.dot(chooser[...], coarse, preferred_element_type=jnp.float32)
    taken = taken + jnp.dot(chooser[...], fine, preferred_element_type=jnp.float32)
    out_ref[:, 0:224] = taken[0:64, 0:224].astype(jnp.bfloat16)
    out_ref[:, 224:448] = taken[64:128, 0:224].astype(jnp.bfloat16)


def per_device(route_group, expert_pick, route_score, expert_hidden, down_weight):
    hbm = pl.BlockSpec(memory_space=pl.ANY)
    return pl.pallas_call(
        kernel,
        out_shape=jax.ShapeDtypeStruct((64, 448), jnp.bfloat16),
        in_specs=[hbm] * 5,
        out_specs=pl.BlockSpec(memory_space=pltpu.VMEM),
        scratch_shapes=[
            pltpu.VMEM((4, 64), jnp.int32),
            pltpu.VMEM((4, 2, 64), jnp.int32),
            pltpu.VMEM((4, 2, 64), jnp.float32),
            pltpu.VMEM((20, 4096), jnp.bfloat16),
            pltpu.VMEM((2, 512, 2048), jnp.bfloat16),
            pltpu.VMEM((2 * NM, ROWS, WIDE), jnp.bfloat16),
            pltpu.VMEM((NG, 1, 2 * LANES), jnp.float32),
            pltpu.VMEM((NG, 1, 2 * LANES), jnp.float32),
            pltpu.VMEM((len(BATCHES), 2, LANES, 512), jnp.float32),
            pltpu.VMEM((NG, 5, 4, LANES), jnp.int32),
            pltpu.VMEM((NG, 5, 4, LANES), jnp.int32),
            pltpu.VMEM((LANES, 20 * NG), jnp.bfloat16),
            pltpu.SemaphoreType.DMA((6,)),
            pltpu.SemaphoreType.DMA,
            pltpu.SemaphoreType.DMA((64,)),
            pltpu.SemaphoreType.DMA,
            pltpu.SemaphoreType.DMA,
            pltpu.SemaphoreType.DMA,
            pltpu.SemaphoreType.DMA,
            pltpu.SemaphoreType.DMA,
            pltpu.SemaphoreType.REGULAR((3,)),
        ],
        compiler_params=pltpu.CompilerParams(
            collective_id=0, has_side_effects=True, vmem_limit_bytes=63 << 20
        ),
        name="experts_return",
    )(
        jnp.transpose(route_group, (1, 0)),
        jnp.transpose(expert_pick, (1, 2, 0)),
        jnp.transpose(route_score, (1, 2, 0)),
        expert_hidden[0],
        jnp.swapaxes(down_weight[0], 1, 2),
    )


def solution(mesh):
    placed = (
        P("group", None),
        P("group", None, None),
        P("group", None, None),
        P("group", "member", None),
        P("group", None, None, "member"),
    )
    return jax.shard_map(
        per_device, mesh=mesh, in_specs=placed, out_specs=P("group", "member"), check_vma=False
    )
```

```python
import functools

import jax
import jax.numpy as jnp
from jax import lax
from jax.experimental import pallas as pl
from jax.experimental.pallas import tpu as pltpu
from jax.sharding import PartitionSpec as P

MESH = pl.DeviceIdType.MESH
NG = 32
NM = 16
ROWS = 8
WIDE = 5120
HALF = WIDE // 2
LANES = 128
MAIN = 64

BATCHES = (
    ((0, 0), (1, 0), (3, 0)),
    ((2, 0), (0, 1), (0, 3)),
    ((1, 1), (3, 1), (1, 3), (3, 3)),
    ((2, 1), (2, 3), (0, 2)),
    ((3, 2), (1, 2)),
    ((2, 2),),
)


def slot_in_batch(half, first, second):
    slot = jnp.int32(0)
    for batch in BATCHES:
        for index, (du, dv) in enumerate(batch):
            here = (first == du) & (second == dv)
            slot = jnp.where(here, index + half * len(batch), slot)
    return slot


def kernel(
    route_hbm, pick_hbm, score_hbm, hidden_hbm, weight_hbm, out_ref,
    route, pick, score, hidden, weight, blocks, table, table_in, products, words, words_in, chooser,
    load_sem, gather_send, gather_recv, table_send, table_recv, word_send, word_recv, own_sem,
    round_sem,
):
    g = lax.axis_index("group")
    m = lax.axis_index("member")
    z, core = g // 2, g % 2
    y, x = m // 4, m % 4

    loads = [
        pltpu.make_async_copy(source, target, load_sem.at[i])
        for i, (source, target) in enumerate(
            (
                (hidden_hbm, hidden),
                (route_hbm, route),
                (pick_hbm, pick),
                (score_hbm, score),
                (weight_hbm.at[:, pl.ds(0, 224), :], weight.at[:, pl.ds(0, 224), :]),
                (weight_hbm.at[:, pl.ds(224, 224), :], weight.at[:, pl.ds(256, 224), :]),
            )
        )
    ]
    for load in loads:
        load.start()

    def member_at(dx, dy):
        return ((y + dy) % 4) * 4 + (x + dx) % 4

    barrier = pltpu.get_barrier_semaphore()
    for dx, dy in ((1, 0), (3, 0), (0, 1), (0, 3)):
        pl.semaphore_signal(barrier, inc=1, device_id=(g, member_at(dx, dy)), device_id_type=MESH)

    def along_z(steps):
        return (g + 2 * steps) % NG

    other_core = g + 1 - 2 * core
    for to in [along_z(steps) for steps in (2, -2, 1, -1)] + [other_core]:
        pl.semaphore_signal(barrier, inc=1, device_id=(to, m), device_id_type=MESH)

    pl.semaphore_wait(barrier, 9)

    def tell(step, targets):
        for to in targets:
            pl.semaphore_signal(round_sem.at[step], inc=1, device_id=(to, m), device_id_type=MESH)

    def told(step, count):
        pl.semaphore_wait(round_sem.at[step], count)

    tell(0, [along_z(steps) for steps in (2, -2, 1, -1)])

    loads[0].wait()
    for half in (0, 1):
        at = 10 * half
        mine = half * NM + m
        blocks[mine, :, 0:4096] = hidden[at : at + 8, :]
        blocks[mine, :, 4096:WIDE] = jnp.concatenate(
            [hidden[at + 8 : at + 10, q * 1024 : (q + 1) * 1024] for q in range(4)], axis=0
        )

    def offsets(half, du, dv):
        return (du, dv) if half == 0 else (dv, du)

    def slot_of(half, du, dv):
        dx, dy = offsets(half, du, dv)
        return half * NM + member_at(dx, dy)

    def part_of(slot, part):
        return blocks.at[slot, :, pl.ds(part * HALF, HALF)]

    def copy(half, du, dv, part, su, sv):
        slot = slot_of(half, du, dv)
        ref = part_of(slot, part)
        index = ((half * 4 + (du - su) % 4) * 4 + (dv - sv) % 4) * 2 + part
        return pltpu.make_async_remote_copy(
            src_ref=ref,
            dst_ref=ref,
            send_sem=gather_send,
            recv_sem=gather_recv.at[index],
            device_id=(g, member_at(*offsets(half, su, sv))),
            device_id_type=MESH,
        )

    def send(half, du, dv, part, su, sv):
        copy(half, du, dv, part, su, sv).start()

    def arrived(half, du, dv, part):
        ref = part_of(slot_of(half, du, dv), part)
        index = ((half * 4 + du) * 4 + dv) * 2 + part
        pltpu.make_async_remote_copy(
            src_ref=ref, dst_ref=ref, send_sem=gather_send, recv_sem=gather_recv.at[index],
            device_id=(g, m), device_id_type=MESH,
        ).wait_recv()

    along = ((1, 0), (3, 0))
    cross = ((0, 1), (0, 3))

    def spread(half, du, dv, parts, targets):
        for part, (su, sv) in zip(parts, targets):
            send(half, du, dv, part, su, sv)

    for parts in ((0, 1), (1, 0)):
        for half in (0, 1):
            spread(half, 0, 0, parts, along)
    for parts in ((0, 1), (1, 0)):
        for half in (0, 1):
            spread(half, 0, 0, parts, cross)

    for load in loads[1:4]:
        load.wait()
    group_row = lax.broadcasted_iota(jnp.int32, (NG, 64), 0)
    chosen = [route[k : k + 1, :] == group_row for k in range(4)]
    per_token = sum(c.astype(jnp.float32) for c in chosen)
    before = (
        lax.broadcasted_iota(jnp.int32, (64, 64), 0) < lax.broadcasted_iota(jnp.int32, (64, 64), 1)
    ).astype(jnp.bfloat16)
    earlier = jnp.dot(per_token.astype(jnp.bfloat16), before, preferred_element_type=jnp.float32)
    ranks = [jnp.sum(jnp.where(c, earlier, 0.0), axis=0, keepdims=True) for c in chosen]
    routes = [route[k : k + 1, :].astype(jnp.float32) for k in range(4)]
    turned = jnp.transpose(jnp.concatenate(ranks + routes, axis=0), (1, 0))

    lane = lax.broadcasted_iota(jnp.int32, (1, LANES), 1)
    dx, dy = (z % 4 - x + 4) % 4, (z // 4 - y + 4) % 4
    slot = slot_in_batch(core, jnp.where(core == 0, dx, dy), jnp.where(core == 0, dy, dx))
    inner = lane % 8
    rank_of_lane = jnp.where(
        lane // 8 == slot, inner, jnp.where(lane // 8 == slot + 8, 8 + inner % 2, -1)
    ).astype(jnp.float32)
    total = jnp.zeros((NG, 2 * LANES), jnp.float32)
    for k in range(4):
        hit = (turned[:, k : k + 1] == rank_of_lane).astype(jnp.float32)
        both = []
        for e in range(2):
            coef = score[k, e : e + 1, :] * pick[k, e : e + 1, :].astype(jnp.float32)
            both.append(
                jnp.dot(
                    jnp.where(chosen[k], coef, 0.0), hit,
                    preferred_element_type=jnp.float32, precision=lax.Precision.HIGHEST,
                )
            )
        total = total + jnp.concatenate(both, axis=1)
    table[...] = total.reshape(NG, 1, 2 * LANES)

    told(0, 4)
    tell(1, [along_z(steps) for steps in (4, -4, 3, -3)])

    row = lax.broadcasted_iota(jnp.int32, (1, 20 * NG), 1)
    piece, inside = (row % 20) // 4, row % 4
    segment = jnp.where(piece == 4, inside // 2, piece // 2)
    rank = jnp.where(piece == 4, 8 + inside % 2, (piece % 2) * 4 + inside)
    key = (10 * (row // 20) + rank).astype(jnp.float32)
    picks = jnp.zeros((64, 20 * NG), jnp.float32)
    for k in range(4):
        token_key = 10.0 * turned[:, 4 + k : 5 + k] + turned[:, k : k + 1]
        picks = picks + (token_key == key).astype(jnp.float32)
    for s in (0, 1):
        chooser[64 * s : 64 * (s + 1), :] = jnp.where(segment == s, picks, 0.0).astype(jnp.bfloat16)

    loads[4].wait()
    loads[5].wait()
    weight[:, 224:256, :] = jnp.zeros((2, 32, 2048), jnp.bfloat16)
    weight[:, 480:512, :] = jnp.zeros((2, 32, 2048), jnp.bfloat16)

    def blocks_of(batch):
        return [(half, du, dv) for half in (0, 1) for du, dv in batch]

    def multiply(number):
        slots = [slot_of(*block) for block in blocks_of(BATCHES[number])]
        rows = 8 * len(slots)
        rest = [blocks[s, :, 4096:WIDE] for s in slots]
        line = lax.broadcasted_iota(jnp.int32, (rows, 1), 0)
        for e in range(2):
            result = None
            for q in (2 * e, 2 * e + 1):
                left = jnp.concatenate(
                    [blocks[s, :, q * 1024 : (q + 1) * 1024] for s in slots] + rest, axis=0
                )
                product = lax.dot_general(
                    left, weight[e, :, (q % 2) * 1024 : (q % 2 + 1) * 1024],
                    (((1,), (1,)), ((), ())), preferred_element_type=jnp.float32,
                )
                wanted = jnp.where((line % 8) // 2 == q, product[rows:], 0.0)
                pair = (product[:rows], wanted)
                result = pair if result is None else [a + b for a, b in zip(result, pair)]
            products[number, e, 0:rows] = result[0]
            products[number, e, MAIN : MAIN + rows] = result[1]

    def finish(number):
        todo = blocks_of(BATCHES[number])
        count = len(todo)
        first_word = sum(2 * len(batch) for batch in BATCHES[:number])
        coefs = None
        for half, du, dv in todo:
            home = 2 * member_at(*offsets(half, du, dv)) + half
            coefs = table_in[home] if coefs is None else coefs + table_in[home]
        rows = [coefs[:, :LANES], coefs[:, LANES:]] * 4
        columns = jnp.transpose(jnp.concatenate(rows, axis=0), (1, 0))

        def weighted(at):
            rows = slice(at, at + 8 * count)
            first = products[number, 0, rows] * columns[rows, 0:1]
            return first + products[number, 1, rows] * columns[rows, 1:2]

        main, tail = weighted(0), weighted(MAIN)
        tail = tail + pltpu.roll(tail, 8 * count - 4, 0)
        tail = tail + pltpu.roll(tail, 8 * count - 2, 0)
        for rows, is_tail in ((main, False), (tail, True)):
            for s in (0, 1):
                values = rows[:, 256 * s : 256 * (s + 1)]
                peak = jnp.max(jnp.abs(values), axis=1, keepdims=True)
                power = jnp.ceil(jnp.log2(jnp.maximum(peak, 1e-30) * (1.0 / 32767.0)))
                fixed = values * jnp.exp2(-power)
                fixed = jnp.clip(jnp.round(fixed), -32767.0, 32767.0).astype(jnp.int32)
                high = jnp.where(lane < 96, fixed[:, LANES:], power.astype(jnp.int32))
                packed = (high << 16) | (fixed[:, :LANES] & 0xFFFF)
                for j in range(count):
                    if is_tail:
                        words[first_word + j, 4, 2 * s : 2 * s + 2, :] = packed[8 * j : 8 * j + 2]
                    else:
                        words[first_word + j, 2 * s] = packed[8 * j : 8 * j + 4]
                        words[first_word + j, 2 * s + 1] = packed[8 * j + 4 : 8 * j + 8]
        for j, (half, du, dv) in enumerate(todo):
            home = 2 * member_at(*offsets(half, du, dv)) + half

            @pl.when(home != g)
            def _():
                pltpu.make_async_remote_copy(
                    src_ref=words.at[first_word + j], dst_ref=words_in.at[g],
                    send_sem=word_send, recv_sem=word_recv,
                    device_id=(home, m), device_id_type=MESH,
                ).start()

            @pl.when(home == g)
            def _():
                pltpu.make_async_copy(words.at[first_word + j], words_in.at[g], own_sem).start()

    def pass_along(half):
        arrived(half, 3, 0, 0)
        arrived(half, 1, 0, 1)
        send(half, 3, 0, 0, 1, 0)
        send(half, 1, 0, 1, 3, 0)

    def pass_cross(half, du):
        arrived(half, du, 3, 0)
        arrived(half, du, 1, 1)
        send(half, du, 3, 0, 0, 1)
        send(half, du, 1, 1, 0, 3)

    def rest_cross(half, du):
        arrived(half, du, 3, 1)
        arrived(half, du, 1, 0)

    def opposite(half, du):
        arrived(half, du, 2, 0)
        arrived(half, du, 2, 1)

    halves = (0, 1)
    for half in halves:
        pass_along(half)
    for half in halves:
        spread(half, 3, 0, (0, 0), cross)
        spread(half, 1, 0, (1, 1), cross[::-1])
    for half in halves:
        arrived(half, 3, 0, 1)
        arrived(half, 1, 0, 0)
        spread(half, 3, 0, (1, 1), cross[::-1])
        spread(half, 1, 0, (0, 0), cross)
    told(1, 4)
    tell(2, [other_core])
    told(2, 1)
    for steps in [sign * steps for steps in range(NG // 2, 0, -1) for sign in (1, -1)][1:]:
        to = (g + steps) % NG
        pltpu.make_async_remote_copy(
            src_ref=table.at[to], dst_ref=table_in.at[g], send_sem=table_send, recv_sem=table_recv,
            device_id=(to, m), device_id_type=MESH,
        ).start()
    table_in[g] = table[g]
    for half in halves:
        pass_cross(half, 0)
    multiply(0)
    for half in halves:
        arrived(half, 2, 0, 0)
        arrived(half, 2, 0, 1)
        spread(half, 2, 0, (0, 1), cross)
        spread(half, 2, 0, (1, 0), cross)
    for du in (0,):
        for half in halves:
            rest_cross(half, du)
    multiply(1)
    for du in (3, 1):
        for half in halves:
            pass_cross(half, du)
    for du in (3, 1):
        for half in halves:
            rest_cross(half, du)
    multiply(2)
    for half in halves:
        pass_cross(half, 2)
    tables = pltpu.make_async_remote_copy(
        src_ref=table.at[pl.ds(0, NG - 1)], dst_ref=table_in.at[pl.ds(0, NG - 1)],
        send_sem=table_send, recv_sem=table_recv, device_id=(g, m), device_id_type=MESH,
    )
    tables.wait_recv()
    finish(0)
    finish(1)
    finish(2)
    for du in (2,):
        for half in halves:
            rest_cross(half, du)
    for du in (0,):
        for half in halves:
            opposite(half, du)
    multiply(3)
    finish(3)
    for du in (3, 1):
        for half in halves:
            opposite(half, du)
    multiply(4)
    finish(4)
    for du in (2,):
        for half in halves:
            opposite(half, du)
    multiply(5)
    finish(5)

    pltpu.make_async_copy(words.at[0], words_in.at[0], own_sem).wait()
    pltpu.make_async_remote_copy(
        src_ref=words.at[pl.ds(0, NG - 1)], dst_ref=words_in.at[pl.ds(0, NG - 1)],
        send_sem=word_send, recv_sem=word_recv, device_id=(g, m), device_id_type=MESH,
    ).wait()

    received = words_in[...].reshape(20 * NG, LANES)
    high = received >> 16
    low = (received << 16) >> 16
    scale = jnp.exp2(high[:, 96:97].astype(jnp.float32))
    values = jnp.concatenate([low, high], axis=1).astype(jnp.float32) * scale
    coarse = values.astype(jnp.bfloat16)
    fine = (values - coarse.astype(jnp.float32)).astype(jnp.bfloat16)
    taken = jnp.dot(chooser[...], coarse, preferred_element_type=jnp.float32)
    taken = taken + jnp.dot(chooser[...], fine, preferred_element_type=jnp.float32)
    out_ref[:, 0:224] = taken[0:64, 0:224].astype(jnp.bfloat16)
    out_ref[:, 224:448] = taken[64:128, 0:224].astype(jnp.bfloat16)

    pltpu.make_async_remote_copy(
        src_ref=blocks.at[pl.ds(0, 30)], dst_ref=blocks.at[pl.ds(0, 30)],
        send_sem=gather_send, recv_sem=gather_recv.at[0], device_id=(g, m), device_id_type=MESH,
    ).wait_send()
    tables.wait_send()


def per_device(route_group, expert_pick, route_score, expert_hidden, down_weight):
    hbm = pl.BlockSpec(memory_space=pl.ANY)
    return pl.pallas_call(
        kernel,
        out_shape=jax.ShapeDtypeStruct((64, 448), jnp.bfloat16),
        in_specs=[hbm] * 5,
        out_specs=pl.BlockSpec(memory_space=pltpu.VMEM),
        scratch_shapes=[
            pltpu.VMEM((4, 64), jnp.int32),
            pltpu.VMEM((4, 2, 64), jnp.int32),
            pltpu.VMEM((4, 2, 64), jnp.float32),
            pltpu.VMEM((20, 4096), jnp.bfloat16),
            pltpu.VMEM((2, 512, 2048), jnp.bfloat16),
            pltpu.VMEM((2 * NM, ROWS, WIDE), jnp.bfloat16),
            pltpu.VMEM((NG, 1, 2 * LANES), jnp.float32),
            pltpu.VMEM((NG, 1, 2 * LANES), jnp.float32),
            pltpu.VMEM((len(BATCHES), 2, LANES, 512), jnp.float32),
            pltpu.VMEM((NG, 5, 4, LANES), jnp.int32),
            pltpu.VMEM((NG, 5, 4, LANES), jnp.int32),
            pltpu.VMEM((LANES, 20 * NG), jnp.bfloat16),
            pltpu.SemaphoreType.DMA((6,)),
            pltpu.SemaphoreType.DMA,
            pltpu.SemaphoreType.DMA((64,)),
            pltpu.SemaphoreType.DMA,
            pltpu.SemaphoreType.DMA,
            pltpu.SemaphoreType.DMA,
            pltpu.SemaphoreType.DMA,
            pltpu.SemaphoreType.DMA,
            pltpu.SemaphoreType.REGULAR((3,)),
        ],
        compiler_params=pltpu.CompilerParams(
            collective_id=0, has_side_effects=True, vmem_limit_bytes=63 << 20
        ),
        name="experts_return",
    )(
        jnp.transpose(route_group, (1, 0)),
        jnp.transpose(expert_pick, (1, 2, 0)),
        jnp.transpose(route_score, (1, 2, 0)),
        expert_hidden[0],
        jnp.swapaxes(down_weight[0], 1, 2),
    )


def solution(mesh):
    placed = (
        P("group", None),
        P("group", None, None),
        P("group", None, None),
        P("group", "member", None),
        P("group", None, None, "member"),
    )
    return jax.shard_map(
        per_device, mesh=mesh, in_specs=placed, out_specs=P("group", "member"), check_vma=False
    )
```
